256 devices in a mesh: sky: 32 (over z, x), exp: 8 (over y, core).
Axes of the slice: x: 4, y: 4, z: 8, core: 2. Of those that a mesh axis runs over, the one named last changes fastest.
Arguments:
- sky_start: float32 [256, 128, 128], P('sky'), may hold values from 0 to 2
- observed: bfloat16 [8, 512, 4, 128, 128], P('exp', 'sky'), may hold values from -6 to 6
- src_owner: int32 [8, 512], P('exp', 'sky'), may hold values from 0 to 31, as said below
- src_local: int32 [8, 512], P('exp', 'sky'), may hold values from 0 to 7
- res_ids: int32 [8, 512, 4], P('exp', 'sky'), may hold values from 0 to 15
- psf_ids: int32 [8, 512, 4], P('exp', 'sky'), may hold values from 0 to 15
- pixel_mask: int32 [8, 512, 4, 2, 128], P('exp', 'sky'), may hold values 0 or 1
- resample: float32 [16, 128, 128], replicated, may hold values from -0.5 to 0.5
- psf: float32 [16, 128, 128], replicated, may hold values from -0.5 to 0.5
Outputs:
- estimate: float32 [256, 128, 128], P('sky')
The draws below stay inside these ranges and needn't reach their ends.
Inputs may be any that keep to these rules, and one draw needn't show every extreme that they name: `src_owner`: each device's 16 footprint rows name any one owner at most 2 times; in every chip set one owner is named 2 times by the rows of every device.
All inputs are finite; a program needn't handle non-finite values. No bound on the sum of `pixel_mask` on one device may be relied on, other than what follows from the above.
Results may differ from the reference program's by a relative error of at most 0.002.
Values may be sent and summed in bfloat16 or wider, within the bound.
A program may use at most 128 MiB of HBM per device.

```python
import jax
import jax.numpy as jnp
from jax import lax

B = 128
SKYBLK_DEV = 8
REQ = 16
EXPO = 4
NRES = 16
NPSF = 16
ITERS = 2
SKYBLK = 256
ROWS = 512
COVER = 64
N_SKY = 32
N_EXP = 8


def draw_src_owner(key, part):
    capacity = max(2, 2 * REQ // N_SKY)
    slot_count = N_SKY * capacity

    def one_device(device):
        chip_set = device // N_SKY
        hottest = jax.random.randint(jax.random.fold_in(key, 7000000 + chip_set), (), 0, N_SKY)
        first_key, second_key = jax.random.split(jax.random.fold_in(key, device))
        shuffled = jax.random.permutation(first_key, slot_count)
        owners = jnp.arange(slot_count) // capacity
        scores = jnp.where(owners == hottest, shuffled - slot_count, shuffled)
        chosen = owners[jnp.argsort(scores)[:REQ]]
        return chosen[jax.random.permutation(second_key, REQ)]
    result = jax.vmap(one_device)(jnp.arange(N_EXP * N_SKY))
    return result.reshape(N_EXP, N_SKY * REQ).astype(jnp.int32)


def set_ends(entries, stream_key, smallest, high):
    longest = entries.shape.index(max(entries.shape))
    spots = []
    for shift in (0, 1):
        where = [jax.random.randint(jax.random.fold_in(stream_key, axis), (), 0, length) for axis, length in enumerate(entries.shape)]
        where[longest] = (where[longest] + shift) % entries.shape[longest]
        spots.append(tuple(where))
    return entries.at[spots[0]].set(smallest).at[spots[1]].set(high)


def block_scale(key, shape, cuts, low, top_value):
    gain = 1.0
    for axis_at, blocks in cuts:
        draws = jax.random.uniform(jax.random.fold_in(jax.random.fold_in(key, 6), axis_at), (blocks,), jnp.float32, low / len(cuts), top_value / len(cuts))
        gain = gain * jnp.repeat(jnp.exp(draws), shape[axis_at] // blocks).reshape((-1,) + (1,) * (len(shape) - 1 - axis_at))
    return gain


def normal_values(stream_key, shape, scale, most, cuts=(), held_as=jnp.bfloat16):
    values = jax.random.normal(stream_key, shape, jnp.float32) * scale
    if len(cuts) > 0:
        values = block_scale(stream_key, shape, cuts, -0.22, 0.18) * values
    return jnp.clip(values, min=-most, max=most).astype(held_as)


def setup_inputs(seed: int = 0) -> dict:
    arg_keys = jax.random.split(jax.random.key(seed), 10)
    sky_start = jnp.clip(2.0 * jax.random.uniform(arg_keys[0], (SKYBLK, B, B), jnp.float32) ** block_scale(arg_keys[0], (SKYBLK, B, B), ((0, 32),), -0.2, 0.2), 0.0, 2.0)
    observed = normal_values(arg_keys[1], (N_EXP, ROWS, EXPO, B, B), 1.0, 6.0, ((0, 8), (1, 32)))
    src_owner = draw_src_owner(jax.random.fold_in(arg_keys[9], 71), 0)
    src_local = set_ends(jax.random.randint(arg_keys[3], (N_EXP, ROWS), 0, SKYBLK_DEV), jax.random.fold_in(arg_keys[3], 1), 0, SKYBLK_DEV - 1).astype(jnp.int32)
    res_ids = set_ends(jax.random.randint(arg_keys[4], (N_EXP, ROWS, EXPO), 0, NRES), jax.random.fold_in(arg_keys[4], 1), 0, NRES - 1).astype(jnp.int32)
    psf_ids = set_ends(jax.random.randint(arg_keys[5], (N_EXP, ROWS, EXPO), 0, NPSF), jax.random.fold_in(arg_keys[5], 1), 0, NPSF - 1).astype(jnp.int32)
    pixel_mask = set_ends((jax.random.randint(arg_keys[6], (N_EXP, ROWS, EXPO, 2, B), 0, 8) < 7).astype(jnp.int32), jax.random.fold_in(arg_keys[6], 1), 0, 1)
    resample = normal_values(arg_keys[7], (NRES, B, B), B ** -0.5, 0.5, (), jnp.float32)
    psf = normal_values(arg_keys[8], (NPSF, B, B), B ** -0.5, 0.5, (), jnp.float32)
    return {"sky_start": sky_start, "observed": observed, "src_owner": src_owner, "src_local": src_local, "res_ids": res_ids, "psf_ids": psf_ids, "pixel_mask": pixel_mask, "resample": resample, "psf": psf}


def project(modeled, observed_blk, resamp_mats, psf_mats, weight):
    hp = lax.Precision.HIGHEST
    inner = jnp.einsum('qeij,qjk->qeik', resamp_mats, modeled, precision=hp)
    predicted = jnp.einsum('qeik,qelk->qeil', inner, psf_mats, precision=hp)
    resid = weight * (predicted - observed_blk.astype(jnp.float32))
    spread = jnp.einsum('qeil,qelk->qeik', resid, psf_mats, precision=hp)
    return jnp.einsum('qeij,qeik->qjk', resamp_mats, spread, precision=hp)


def reference(sky_start, observed, src_owner, src_local, res_ids, psf_ids, pixel_mask, resample, psf):
    groups = N_EXP * N_SKY
    sources = (src_owner * SKYBLK_DEV + src_local).astype(jnp.int32).reshape(groups, REQ)
    obs_all = observed.reshape(groups, REQ, EXPO, B, B)
    res_all = res_ids.reshape(groups, REQ, EXPO)
    psf_all = psf_ids.reshape(groups, REQ, EXPO)
    mask_all = pixel_mask.reshape(groups, REQ, EXPO, 2, B)
    step_size = 1.0 / (2.0 * float(COVER))
    estimate = sky_start
    for iteration in range(ITERS):
        model_all = lax.optimization_barrier(estimate.astype(jnp.bfloat16)).astype(jnp.float32)

        def one_group(total, inputs):
            src_rows, obs_rows, res_rows, psf_rows, mask_rows = inputs
            masks = mask_rows.astype(jnp.float32)
            weight = masks[:, :, 0, :, None] * masks[:, :, 1, None, :]
            back_proj = project(model_all[src_rows], obs_rows, resample[res_rows], psf[psf_rows], weight)
            return total.at[src_rows].add(back_proj), None

        grad, _ = lax.scan(one_group, jnp.zeros(estimate.shape, jnp.float32), (sources, obs_all, res_all, psf_all, mask_all))
        estimate = jnp.maximum(estimate - step_size * grad, 0.0)
    return estimate
```

```python
import functools

import jax
import jax.numpy as jnp
from jax import lax
from jax.experimental import pallas as pl
from jax.experimental.pallas import tpu as pltpu
from jax.sharding import PartitionSpec as P

MESH = pl.DeviceIdType.MESH
BF = jnp.bfloat16
F32 = jnp.float32
I32 = jnp.int32
ITERS = 2
NZ, NRING = 8, 4
B = 128
H = 64
REQ = 16
EXPO = 4
STEP = 1.0 / 128.0
ORDER = (0, 1, 3, 2)
POS = {0: 0, 1: 1, 3: 2, 2: 3}


def coords():
    s = lax.axis_index("sky")
    e = lax.axis_index("exp")
    return s // NRING, s % NRING, e // 2, e % 2


def at(z, x, y, c):
    return (z * NRING + x, y * 2 + c)


class Net:
    def __init__(self, send, recv):
        self.send, self.recv, self.used, self.open = send, recv, 0, []
        self.z, self.x, self.y, self.c = coords()

    def along(self, axis, k):
        z, x, y, c = self.z, self.x, self.y, self.c
        if axis == "z":
            return at((z + k) % NZ, x, y, c)
        if axis == "x":
            return at(z, (x + k) % NRING, y, c)
        if axis == "y":
            return at(z, x, (y + k) % NRING, c)
        return at(z, x, y, 1 - c)

    def copy(self, src, dst, axis, k):
        i = self.used
        self.used += 1
        cp = pltpu.make_async_remote_copy(
            src_ref=src, dst_ref=dst, send_sem=self.send.at[i], recv_sem=self.recv.at[i],
            device_id=self.along(axis, k), device_id_type=MESH)
        cp.start()
        self.open.append(cp)
        return cp

    def barrier(self):
        bar = pltpu.get_barrier_semaphore()
        peers = [self.along("c", 1)]
        peers += [self.along(a, k) for a in ("x", "y") for k in (1, 2, 3)]
        peers += [self.along("z", k) for k in range(1, NZ)]
        for peer in peers:
            pl.semaphore_signal(bar, inc=1, device_id=peer, device_id_type=MESH)
        pl.semaphore_wait(bar, len(peers))

    def drain(self):
        for cp in self.open:
            cp.wait_send()


HALVES = (("x", "y", 0), ("y", "x", H))


def ring_at(net, axis):
    return net.x if axis == "x" else net.y


def gather(net, block, gz, full, slots, got, tabs, ids, out):
    gz[net.z] = block
    zc = {k: net.copy(gz.at[net.z], gz.at[net.z], "z", k) for k in (4, 3, 5, 2, 6, 1, 7)}
    for k in (1, 7, 2, 6, 3, 5, 4):
        zc[k].wait_recv()
    mid, cores = {}, []
    for k in (2, 1, 3):
        for h, (dense, _, lo) in enumerate(HALVES):
            here = pl.ds(net.c * 32 + ring_at(net, dense) * NZ, NZ)
            mid[h, k] = net.copy(gz.at[:, pl.ds(lo, H)], full[h].at[here], dense, k)
    for h, (dense, _, lo) in enumerate(HALVES):
        here = pl.ds(net.c * 32 + ring_at(net, dense) * NZ, NZ)
        cores.append(net.copy(gz.at[:, pl.ds(lo, H)], full[h].at[here], "c", 1))
        full[h][here] = gz[:, lo:lo + H]
    for k in (1, 3, 2):
        for h, (dense, _, lo) in enumerate(HALVES):
            mid[h, k].wait_recv()
            there = pl.ds(net.c * 32 + ((ring_at(net, dense) - k + NRING) % NRING) * NZ, NZ)
            cores.append(net.copy(full[h].at[there], full[h].at[there], "c", 1))
    for cp in cores:
        cp.wait_recv()
    last = {}
    for k in (2, 1, 3, 0):
        for h, (_, sparse, lo) in enumerate(HALVES):
            base = POS[(NRING - k) % NRING] * REQ
            mine = ring_at(net, sparse)

            def fill(r, carry, h=h, k=k, base=base, mine=mine):
                half = full[h][tabs[4 + h, base + r]]
                if k == 0:
                    got[h][mine, r] = half
                else:
                    slots[h][k, r] = half
                return carry

            lax.fori_loop(0, REQ, fill, 0, unroll=4)
            if k:
                last[h, k] = net.copy(slots[h].at[k], got[h].at[mine], sparse, k)
    for k in (1, 3, 2):
        for h in range(2):
            last[h, k].wait_recv()

    def place(r, carry):
        row = ids[r]
        out[r, 0:H] = got[0][(row // 2) % NRING, r]
        out[r, H:B] = got[1][(row // 8) % NRING, r]
        return carry

    lax.fori_loop(0, REQ, place, 0, unroll=4)


def scatter(net, back, rows, cum, core_out, core_in, ring_out, ring_own, ring_in, zout, zown, zin, tabs):
    first, cores, mids = {}, {}, {}
    for k in (2, 1, 3):
        for h, (_, sparse, lo) in enumerate(HALVES):
            first[h, k] = net.copy(back.at[:, pl.ds(lo, H)], rows[h].at[k], sparse, k)
    for k in ORDER:
        for h, (_, sparse, lo) in enumerate(HALVES):
            if k:
                first[h, k].wait_recv()

            def add(r, carry, h=h, k=k, lo=lo):
                p = POS[k] * REQ + r
                prev = tabs[2 * h, p]
                term = back[r, lo:lo + H] if k == 0 else rows[h][k, r]
                before = cum[h][jnp.maximum(prev, 0)]
                cum[h][p] = term.astype(F32) + jnp.where(prev >= 0, before, 0.0)
                return carry

            lax.fori_loop(0, REQ, add, 0, unroll=4)

    def total(h, key):
        at_last = tabs[2 * h + 1, key]
        return jnp.where(at_last >= 0, cum[h][jnp.maximum(at_last, 0)], 0.0)

    for k in (2, 1, 3, 0):
        for h, (dense, _, lo) in enumerate(HALVES):
            there = (ring_at(net, dense) + k) % NRING

            def pick(z, carry, h=h, k=k, there=there):
                core_out[h][k, z] = total(h, (1 - net.c) * 32 + there * NZ + z).astype(BF)
                return carry

            lax.fori_loop(0, NZ, pick, 0, unroll=4)
            cores[h, k] = net.copy(core_out[h].at[k], core_in[h].at[k], "c", 1)
    for k in (2, 1, 3, 0):
        for h, (dense, _, lo) in enumerate(HALVES):
            cores[h, k].wait_recv()
            there = (ring_at(net, dense) + k) % NRING

            def join(z, carry, h=h, k=k, there=there):
                both = total(h, net.c * 32 + there * NZ + z) + core_in[h][k, z].astype(F32)
                if k:
                    ring_out[h][k, z] = both.astype(BF)
                else:
                    ring_own[h][z] = both
                return carry

            lax.fori_loop(0, NZ, join, 0, unroll=4)
            if k:
                mids[h, k] = net.copy(ring_out[h].at[k], ring_in[h].at[k], dense, k)
    for h in range(2):
        for k in (1, 3, 2):
            mids[h, k].wait_recv()
    for h, (_, _, lo) in enumerate(HALVES):

        def ring(z, carry, h=h, lo=lo):
            both = ring_own[h][z]
            for k in (1, 3, 2):
                both = both + ring_in[h][k, z].astype(F32)
            zout[z, lo:lo + H] = both.astype(BF)
            zown[z, lo:lo + H] = both
            return carry

        lax.fori_loop(0, NZ, ring, 0, unroll=4)
    zc = {k: net.copy(zout.at[(net.z + k) % NZ], zin.at[k], "z", k) for k in (4, 3, 5, 2, 6, 1, 7)}
    grad = zown[net.z]
    for k in (1, 7, 2, 6, 3, 5, 4):
        zc[k].wait_recv()
        grad = grad + zin[k].astype(F32)
    return grad


def tables(net, seen, tab_ref):
    lane = lax.broadcasted_iota(I32, (B, B), 1)
    sub = lax.broadcasted_iota(I32, (B, B), 0)
    for h in range(2):
        ids = sum(seen[h, k, POS[k]:POS[k] + 1, :] for k in range(NRING))
        zz, xx, yy, cc = ids // 32, (ids // 8) % 4, (ids // 2) % 4, ids % 2
        ring = xx if h == 0 else yy
        index = cc * 32 + ring * NZ + zz
        mine = (yy == net.y) if h == 0 else (xx == net.x)
        real = lane[0:1] < NRING * REQ
        key = jnp.where(jnp.logical_and(mine, real), index, -1).astype(F32)
        column = jnp.sum(jnp.where(lane == sub, jnp.broadcast_to(key, (B, B)), 0.0), axis=1, keepdims=True)
        same = jnp.logical_and(column == key, column >= 0.0)
        earlier = jnp.logical_and(same, sub < lane)
        prev = jnp.max(jnp.where(earlier, sub.astype(F32), -1.0), axis=0, keepdims=True)
        final = jnp.max(jnp.where(column == lane.astype(F32), sub.astype(F32), -1.0), axis=0, keepdims=True)
        tab_ref[2 * h:2 * h + 1, :] = prev.astype(I32)
        tab_ref[2 * h + 1:2 * h + 2, :] = final.astype(I32)
        tab_ref[4 + h:5 + h, :] = index
    tab_ref[6:8, :] = jnp.zeros((2, B), I32)


GATHER = [
    pltpu.VMEM((NZ, B, B), BF),
    pltpu.VMEM((64, H, B), BF), pltpu.VMEM((64, H, B), BF),
    pltpu.VMEM((NRING, REQ, H, B), BF), pltpu.VMEM((NRING, REQ, H, B), BF),
    pltpu.VMEM((NRING, REQ, H, B), BF), pltpu.VMEM((NRING, REQ, H, B), BF),
]
SCATTER = [
    pltpu.VMEM((NRING, REQ, H, B), BF), pltpu.VMEM((NRING, REQ, H, B), BF),
    pltpu.VMEM((64, H, B), F32), pltpu.VMEM((64, H, B), F32),
    pltpu.VMEM((NRING, NZ, H, B), BF), pltpu.VMEM((NRING, NZ, H, B), BF),
    pltpu.VMEM((NRING, NZ, H, B), BF), pltpu.VMEM((NRING, NZ, H, B), BF),
    pltpu.VMEM((NRING, NZ, H, B), BF), pltpu.VMEM((NRING, NZ, H, B), BF),
    pltpu.VMEM((NZ, H, B), F32), pltpu.VMEM((NZ, H, B), F32),
    pltpu.VMEM((NRING, NZ, H, B), BF), pltpu.VMEM((NRING, NZ, H, B), BF),
    pltpu.VMEM((NZ, B, B), BF), pltpu.VMEM((NZ, B, B), F32), pltpu.VMEM((NZ, B, B), BF),
]


def sems(n):
    return [pltpu.SemaphoreType.DMA((n,)), pltpu.SemaphoreType.DMA((n,))]


def pair(refs, i):
    return (refs[i], refs[i + 1])


def unpack_gather(refs):
    return refs[0], pair(refs, 1), pair(refs, 3), pair(refs, 5)


def unpack_scatter(refs):
    return (pair(refs, 0), pair(refs, 2), pair(refs, 4), pair(refs, 6), pair(refs, 8),
            pair(refs, 10), pair(refs, 12), refs[14], refs[15], refs[16])


def first_kernel(sky, idtile, ids, model, tab, seen, tab_smem, local_sem, send, recv, *refs):
    gz, full, slots, got = unpack_gather(refs)
    net = Net(send, recv)
    net.barrier()
    told = []
    for h, (_, sparse, _) in enumerate(HALVES):
        seen[h, 0] = idtile[...]
        for k in (1, 2, 3):
            told.append(net.copy(idtile, seen.at[h, k], sparse, k))
    for cp in told:
        cp.wait_recv()
    tables(net, seen, tab)
    cp = pltpu.make_async_copy(tab, tab_smem, local_sem)
    cp.start()
    cp.wait()
    block = sky[net.y * 2 + net.c].astype(BF)
    gather(net, block, gz, full, slots, got, tab_smem, ids, model)
    net.drain()


def between_kernel(back, sky, tabs, ids, model, estimate, send, recv, *refs):
    gz, full, slots, got = unpack_gather(refs[:7])
    net = Net(send, recv)
    net.barrier()
    grad = scatter(net, back, *unpack_scatter(refs[7:]), tabs)
    new = jnp.maximum(sky[net.y * 2 + net.c] - STEP * grad, 0.0)
    estimate[...] = new
    gather(net, new.astype(BF), gz, full, slots, got, tabs, ids, model)
    net.drain()


def last_kernel(back, estimate, tabs, out, held, send, recv, *refs):
    net = Net(send, recv)
    net.barrier()
    grad = scatter(net, back, *unpack_scatter(refs), tabs)
    mine = net.y * 2 + net.c
    held[mine] = jnp.maximum(estimate[...] - STEP * grad, 0.0)
    ring = {k: net.copy(held.at[mine], held.at[mine], "y", k) for k in (2, 1, 3)}
    cores = [net.copy(held.at[mine], held.at[mine], "c", 1)]
    for k in (1, 3, 2):
        ring[k].wait_recv()
        there = ((net.y - k + NRING) % NRING) * 2 + net.c
        cores.append(net.copy(held.at[there], held.at[there], "c", 1))
    for cp in cores:
        cp.wait_recv()
    out[...] = held[...]
    net.drain()


VM = pl.BlockSpec(memory_space=pltpu.VMEM)
SM = pl.BlockSpec(memory_space=pltpu.SMEM)


def params(cid):
    return pltpu.CompilerParams(collective_id=cid, has_side_effects=True, vmem_limit_bytes=56 * 2**20)


ROWS_STEP = 2


def project_kernel(res, psf, model, obs, mask, rm, rt, pm, pt, out):
    step = pl.program_id(0)
    for q in range(ROWS_STEP):
        r_ids = [res[(step * ROWS_STEP + q) * EXPO + x] for x in range(EXPO)]
        p_ids = [psf[(step * ROWS_STEP + q) * EXPO + x] for x in range(EXPO)]
        rows = jnp.concatenate([rm[i] for i in r_ids], axis=0)
        inner = jnp.dot(rows, model[q], preferred_element_type=F32).astype(BF)
        spread, cols = [], []
        for x in range(EXPO):
            predicted = jnp.dot(inner[x * B:(x + 1) * B], pt[p_ids[x]], preferred_element_type=F32)
            good = mask[q, x].astype(F32)
            resid = (predicted - obs[q, x].astype(F32)) * good[1:2]
            spread.append(jnp.dot(resid.astype(BF), pm[p_ids[x]], preferred_element_type=F32).astype(BF))
            cols.append(rt[r_ids[x]] * good[0:1].astype(BF))
        out[q] = jnp.dot(jnp.concatenate(cols, axis=1), jnp.concatenate(spread, axis=0),
                         preferred_element_type=F32).astype(BF)


def project(res, psf, model, obs, mask, rm, rt, pm, pt):
    table = pl.BlockSpec((16, B, B), lambda i, *_: (0, 0, 0))
    return pl.pallas_call(
        project_kernel, name="project",
        grid_spec=pltpu.PrefetchScalarGridSpec(
            num_scalar_prefetch=2, grid=(REQ // ROWS_STEP,),
            in_specs=[
                pl.BlockSpec((ROWS_STEP, B, B), lambda i, *_: (i, 0, 0)),
                pl.BlockSpec((ROWS_STEP, EXPO, B, B), lambda i, *_: (i, 0, 0, 0)),
                pl.BlockSpec((ROWS_STEP, EXPO, 2, B), lambda i, *_: (i, 0, 0, 0)),
                table, table, table, table],
            out_specs=pl.BlockSpec((ROWS_STEP, B, B), lambda i, *_: (i, 0, 0))),
        out_shape=jax.ShapeDtypeStruct((REQ, B, B), BF),
        compiler_params=pltpu.CompilerParams(vmem_limit_bytes=32 * 2**20),
    )(res, psf, model, obs, mask, rm, rt, pm, pt)


def on_device(sky, observed, src_owner, src_local, res_ids, psf_ids, pixel_mask, resample, psf):
    ids = src_owner[0] * 8 + src_local[0]
    idtile = jnp.zeros((8, B), I32)
    for j in range(NRING):
        idtile = idtile.at[j, j * REQ:(j + 1) * REQ].set(ids)
    rm, pm = resample.astype(BF), psf.astype(BF)
    rt, pt = rm.transpose(0, 2, 1), pm.transpose(0, 2, 1)
    model_shape = jax.ShapeDtypeStruct((REQ, B, B), BF)
    model, tabs = pl.pallas_call(
        first_kernel, name="first_gather",
        out_shape=(model_shape, jax.ShapeDtypeStruct((8, B), I32)),
        in_specs=[VM, VM, SM], out_specs=(VM, VM),
        scratch_shapes=[pltpu.VMEM((2, NRING, 8, B), I32), pltpu.SMEM((8, B), I32),
                        pltpu.SemaphoreType.DMA] + sems(40) + GATHER,
        compiler_params=params(0))(sky, idtile, ids)
    fixed = (observed[0], pixel_mask[0], rm, rt, pm, pt)
    res, pids = res_ids[0].reshape(-1), psf_ids[0].reshape(-1)
    back = project(res, pids, model, *fixed)
    model, estimate = pl.pallas_call(
        between_kernel, name="reduce_gather",
        out_shape=(model_shape, jax.ShapeDtypeStruct((B, B), F32)),
        in_specs=[VM, VM, SM, SM], out_specs=(VM, VM),
        scratch_shapes=sems(64) + GATHER + SCATTER,
        compiler_params=params(1))(back, sky, tabs, ids)
    back = project(res, pids, model, *fixed)
    return pl.pallas_call(
        last_kernel, name="reduce_last",
        out_shape=jax.ShapeDtypeStruct((8, B, B), F32),
        in_specs=[VM, VM, SM], out_specs=VM,
        scratch_shapes=[pltpu.VMEM((8, B, B), F32)] + sems(40) + SCATTER,
        compiler_params=params(2))(back, estimate, tabs)


def solution(mesh):
    in_specs = (
        P("sky", None, None),
        P("exp", "sky", None, None, None),
        P("exp", "sky"),
        P("exp", "sky"),
        P("exp", "sky", None),
        P("exp", "sky", None),
        P("exp", "sky", None, None, None),
        P(),
        P(),
    )
    return jax.shard_map(
        on_device, mesh=mesh, in_specs=in_specs, out_specs=P("sky", None, None), check_vma=False
    )
```

```python
import jax
import jax.numpy as jnp
from jax import lax
from jax.experimental import pallas as pl
from jax.experimental.pallas import tpu as pltpu
from jax.sharding import PartitionSpec as P

MESH = pl.DeviceIdType.MESH
BF = jnp.bfloat16
F32 = jnp.float32
I32 = jnp.int32
ITERS = 2
NZ, NRING = 8, 4
B = 128
HALF = 64
CH = 32
REQ = 16
GROUP = 8
EXPO = 4
STEP = 1.0 / 128.0
ORDER = (0, 1, 3, 2)
POS = {0: 0, 1: 1, 3: 2, 2: 3}
FAR = (2, 1, 3)
NEAR = (1, 3, 2)
ZFAR = (4, 3, 5, 2, 6, 1, 7)
ZNEAR = (1, 7, 2, 6, 3, 5, 4)
HALVES = (("x", "y", 0), ("y", "x", HALF))
SEMS = 160


def at(z, x, y, c):
    return (z * NRING + x, y * 2 + c)


class Net:
    def __init__(self, send, recv):
        self.send, self.recv, self.used, self.open = send, recv, 0, []
        s, e = lax.axis_index("sky"), lax.axis_index("exp")
        self.z, self.x, self.y, self.c = s // NRING, s % NRING, e // 2, e % 2
        self.own = e

    def along(self, axis, k):
        z, x, y, c = self.z, self.x, self.y, self.c
        if axis == "z":
            return at((z + k) % NZ, x, y, c)
        if axis == "x":
            return at(z, (x + k) % NRING, y, c)
        if axis == "y":
            return at(z, x, (y + k) % NRING, c)
        return at(z, x, y, 1 - c)

    def on(self, axis):
        return self.x if axis == "x" else self.y

    def copy(self, src, dst, axis, k):
        i = self.used
        self.used += 1
        cp = pltpu.make_async_remote_copy(
            src_ref=src, dst_ref=dst, send_sem=self.send.at[i], recv_sem=self.recv.at[i],
            device_id=self.along(axis, k), device_id_type=MESH)
        cp.start()
        self.open.append(cp)
        return cp

    def barrier(self):
        bar = pltpu.get_barrier_semaphore()
        peers = [self.along("c", 1)]
        peers += [self.along(a, k) for a in ("x", "y") for k in (1, 2, 3)]
        peers += [self.along("z", k) for k in range(1, NZ)]
        for peer in peers:
            pl.semaphore_signal(bar, inc=1, device_id=peer, device_id_type=MESH)
        pl.semaphore_wait(bar, len(peers))


def tables(net, seen, tab):
    lane = lax.broadcasted_iota(I32, (B, B), 1)
    sub = lax.broadcasted_iota(I32, (B, B), 0)
    for h in range(2):
        ids = sum(seen[h, k, POS[k]:POS[k] + 1, :] for k in range(NRING))
        zz, xx, yy, cc = ids // 32, (ids // 8) % 4, (ids // 2) % 4, ids % 2
        ring = xx if h == 0 else yy
        index = cc * 32 + ring * NZ + zz
        mine = (yy == net.y) if h == 0 else (xx == net.x)
        real = lane[0:1] < NRING * REQ
        key = jnp.broadcast_to(jnp.where(jnp.logical_and(mine, real), index, -1), (B, B))
        other = key.T
        earlier = jnp.logical_and(jnp.logical_and(key == other, key >= 0), sub < lane)
        tab[2 * h:2 * h + 1, :] = jnp.max(jnp.where(earlier, sub, -1), axis=0, keepdims=True)
        tab[2 * h + 1:2 * h + 2, :] = jnp.max(jnp.where(other == lane, sub, -1), axis=0, keepdims=True)
        tab[4 + h:5 + h, :] = index
    tab[6:8, :] = jnp.zeros((2, B), I32)


def wait_sends(copies):
    for cp in copies:
        cp.wait_send()


def id_tile(ids):
    lane = lax.broadcasted_iota(I32, (8, B), 1)
    sub = lax.broadcasted_iota(I32, (8, B), 0)
    tile = jnp.zeros((8, B), I32)
    for r, block in enumerate(ids):
        spot = (r // GROUP) * NRING * GROUP + sub * GROUP + r % GROUP
        tile = jnp.where(jnp.logical_and(lane == spot, sub < NRING), block, tile)
    return tile


def place(group, k, r):
    return group * NRING * GROUP + POS[k] * GROUP + r


def send_block(net, est, gz, q):
    gz[q, net.z] = est[q].astype(BF)
    return {k: net.copy(gz.at[q, net.z], gz.at[q, net.z], "z", k) for k in ZFAR}


def gather(net, zc, gz, full, slots, got, tabs):
    mid, cores, last = {}, {0: [], 1: []}, {0: [], 1: []}
    for q in range(2):
        for k in ZNEAR:
            zc[q][k].wait_recv()
        for k in FAR:
            for h, (dense, _, _) in enumerate(HALVES):
                here = pl.ds(net.c * 32 + net.on(dense) * NZ, NZ)
                mid[q, h, k] = net.copy(gz.at[q, :, pl.ds(h * CH, CH)], full[h][q].at[here], dense, k)
        for h, (dense, _, _) in enumerate(HALVES):
            here = pl.ds(net.c * 32 + net.on(dense) * NZ, NZ)
            cores[q].append(net.copy(gz.at[q, :, pl.ds(h * CH, CH)], full[h][q].at[here], "c", 1))
            full[h][q][here] = gz[q, :, h * CH:(h + 1) * CH]

    def slot(group, q):
        for k in FAR + (0,):
            back_k = (NRING - k) % NRING

            def fill(r, carry):
                for h, (_, sparse, _) in enumerate(HALVES):
                    piece = full[h][q][jnp.clip(tabs[4 + h, place(group, back_k, r)], 0, 63)]
                    if k == 0:
                        got[h][group][net.on(sparse), q, r] = piece
                    else:
                        slots[h][k, q, group * GROUP + r] = piece
                return carry

            lax.fori_loop(0, GROUP, fill, 0, unroll=GROUP)
            if k:
                part = pl.ds(group * GROUP, GROUP)
                for h, (_, sparse, _) in enumerate(HALVES):
                    last[group].append(net.copy(
                        slots[h].at[k, q, part], got[h][group].at[net.on(sparse), q], sparse, k))

    for q in range(2):
        for k in NEAR:
            for h, (dense, _, _) in enumerate(HALVES):
                mid[q, h, k].wait_recv()
                there = pl.ds(net.c * 32 + ((net.on(dense) - k + NRING) % NRING) * NZ, NZ)
                cores[q].append(net.copy(full[h][q].at[there], full[h][q].at[there], "c", 1))
        for cp in cores[q]:
            cp.wait_recv()
        slot(0, q)
    for q in range(2):
        slot(1, q)
    return last


def products(group, got, back, owner, inner_id, res, psf, obs, mask, rm, rt, pm, pt):
    def row(i):
        r = group * GROUP + i
        ysrc, xsrc = (inner_id[0, r] // 2) % NRING, owner[0, r] % NRING
        model = jnp.concatenate(
            [got[0][group][ysrc, 0, i], got[0][group][ysrc, 1, i],
             got[1][group][xsrc, 0, i], got[1][group][xsrc, 1, i]], axis=0)
        r_ids = [res[x, r] for x in range(EXPO)]
        p_ids = [psf[x, r] for x in range(EXPO)]
        rows = jnp.concatenate([rm[i] for i in r_ids], axis=0)
        inner = jnp.dot(rows, model, preferred_element_type=F32).astype(BF)
        spread, cols = [], []
        for x in range(EXPO):
            predicted = jnp.dot(inner[x * B:(x + 1) * B], pt[p_ids[x]], preferred_element_type=F32)
            good = mask[r, x].astype(F32)
            resid = (predicted - obs[r, x].astype(F32)) * good[1:2]
            spread.append(jnp.dot(resid.astype(BF), pm[p_ids[x]], preferred_element_type=F32).astype(BF))
            cols.append(rt[r_ids[x]] * good[0:1].astype(BF))
        back[r] = jnp.dot(jnp.concatenate(cols, axis=1), jnp.concatenate(spread, axis=0),
                          preferred_element_type=F32).astype(BF)

    def two(i, carry):
        row(2 * i)
        row(2 * i + 1)
        return carry

    lax.fori_loop(0, GROUP // 2, two, 0)


def send_rows(net, group, back, rows):
    part, copies = pl.ds(group * GROUP, GROUP), {}
    for q in range(2) if group else range(1):
        for k in FAR:
            for h, (_, sparse, lo) in enumerate(HALVES):
                if group:
                    copies[q, h, k] = net.copy(back.at[part, pl.ds(lo + q * CH, CH)],
                                               rows[h].at[k, part, pl.ds(q * CH, CH)], sparse, k)
                else:
                    copies[q, h, k] = net.copy(back.at[part, pl.ds(lo, HALF)], rows[h].at[k, part], sparse, k)
    return copies


def scatter(net, copies, back, rows, cum, core_out, core_in, ring_out, ring_own, ring_in,
            zout, zown, zin, est, tabs, done):
    def accumulate(group, chunks):
        for k in ORDER:
            if k:
                for q in chunks if group else range(1):
                    for h in range(2):
                        copies[group][q, h, k].wait_recv()

            def add(i, carry):
                p, r = place(group, k, i), group * GROUP + i
                for h, (_, _, lo) in enumerate(HALVES):
                    prev = tabs[2 * h, p]
                    for q in chunks:
                        if k == 0:
                            term = back[r, lo + q * CH:lo + (q + 1) * CH]
                        else:
                            term = rows[h][k, r, q * CH:(q + 1) * CH]
                        before = cum[h][q, jnp.clip(prev, 0, 63)]
                        cum[h][q, p] = term.astype(F32) + jnp.where(prev >= 0, before, 0.0)
                return carry

            lax.fori_loop(0, GROUP, add, 0, unroll=GROUP)

    def total(h, q, key):
        final = tabs[2 * h + 1, key]
        return jnp.where(final >= 0, cum[h][q, jnp.clip(final, 0, 63)], 0.0)

    cores, mids = {}, {}

    def to_core(q):
        for k in FAR + (0,):

            def pick(z, carry):
                for h, (dense, _, _) in enumerate(HALVES):
                    there = (net.on(dense) + k) % NRING
                    core_out[h][q, k, z] = total(h, q, (1 - net.c) * 32 + there * NZ + z).astype(BF)
                return carry

            lax.fori_loop(0, NZ, pick, 0, unroll=NZ)
            for h in range(2):
                cores[q, h, k] = net.copy(core_out[h].at[q, k], core_in[h].at[q, k], "c", 1)

    def to_ring(q):
        for k in FAR + (0,):
            for h in range(2):
                cores[q, h, k].wait_recv()

            def join(z, carry):
                for h, (dense, _, _) in enumerate(HALVES):
                    there = (net.on(dense) + k) % NRING
                    both = total(h, q, net.c * 32 + there * NZ + z) + core_in[h][q, k, z].astype(F32)
                    if k:
                        ring_out[h][q, k, z] = both.astype(BF)
                    else:
                        ring_own[h][q, z] = both
                return carry

            lax.fori_loop(0, NZ, join, 0, unroll=NZ)
            if k:
                for h, (dense, _, _) in enumerate(HALVES):
                    mids[q, h, k] = net.copy(ring_out[h].at[q, k], ring_in[h].at[q, k], dense, k)

    accumulate(0, (0, 1))
    for q in range(2):
        accumulate(1, (q,))
        to_core(q)
        to_ring(q)
    zc = {}
    for q in range(2):
        for k in NEAR:
            for h in range(2):
                mids[q, h, k].wait_recv()

        def ring(z, carry):
            for h in range(2):
                both = ring_own[h][q, z]
                for k in NEAR:
                    both = both + ring_in[h][q, k, z].astype(F32)
                zout[q, z, h * CH:(h + 1) * CH] = both.astype(BF)
                zown[q, z, h * CH:(h + 1) * CH] = both
            return carry

        lax.fori_loop(0, NZ, ring, 0, unroll=NZ)
        zc[q] = {k: net.copy(zout.at[q, (net.z + k) % NZ], zin.at[q, k], "z", k) for k in ZFAR}
    for q in range(2):
        grad = zown[q, net.z]
        for k in ZNEAR:
            zc[q][k].wait_recv()
            grad = grad + zin[q, k].astype(F32)
        est[q] = jnp.maximum(est[q] - STEP * grad, 0.0)
        done(q)


def kernel(owner, inner_id, res, psf, mask, sky, observed, resample, psf_mats, out,
           idtile, seen, tab, tabs, r32, p32, rm, rt, pm, pt, obs, est, held, local, send, recv,
           gz, full_a0, full_a1, full_b0, full_b1, slots_a, slots_b, got_a0, got_a1, got_b0, got_b1, back, rows_a, rows_b, cum_a, cum_b,
           co_a, co_b, ci_a, ci_b, ro_a, ro_b, rw_a, rw_b, ri_a, ri_b, zout, zown, zin):
    full, got = ((full_a0, full_a1), (full_b0, full_b1)), ((got_a0, got_a1), (got_b0, got_b1))
    slots, rows = (slots_a, slots_b), (rows_a, rows_b)
    cum, core_out, core_in = (cum_a, cum_b), (co_a, co_b), (ci_a, ci_b)
    ring_out, ring_own, ring_in = (ro_a, ro_b), (rw_a, rw_b), (ri_a, ri_b)
    net = Net(send, recv)

    def fetch(src, dst, i):
        cp = pltpu.make_async_copy(src, dst, local.at[i])
        cp.start()
        return cp

    starts = [fetch(sky.at[net.own, pl.ds(h * HALF + q * CH, CH)], est.at[q, pl.ds(h * CH, CH)], 2 * h + q)
              for q in range(2) for h in range(2)]
    mats = [fetch(resample, r32, 4), fetch(psf_mats, p32, 5)]
    blocks = fetch(observed, obs, 6)
    own_ids = [owner[0, r] * 8 + inner_id[0, r] for r in range(REQ)]
    idtile[...] = id_tile(own_ids)
    net.barrier()
    told = []
    for h, (_, sparse, _) in enumerate(HALVES):
        for k in (1, 2, 3):
            told.append(net.copy(idtile, seen.at[h, k], sparse, k))
        seen[h, 0] = idtile[...]
    for cp in starts:
        cp.wait()
    zc = {q: send_block(net, est, gz, q) for q in range(2)}
    for cp in told:
        cp.wait_recv()
    tables(net, seen, tab)
    to_scalar = fetch(tab, tabs, 7)
    for cp in mats:
        cp.wait()

    def cast(i, carry):
        rm[i] = r32[i].astype(BF)
        rt[i] = r32[i].T.astype(BF)
        pm[i] = p32[i].astype(BF)
        pt[i] = p32[i].T.astype(BF)
        return carry

    lax.fori_loop(0, 16, cast, 0, unroll=2)
    to_scalar.wait()
    first = net.used
    for iteration in range(ITERS):
        last = gather(net, zc, gz, full, slots, got, tabs)
        if iteration == 0:
            blocks.wait()
        gathering, net.open = net.open, []
        copies = {}
        for group in range(2):
            for cp in last[group]:
                cp.wait_recv()
            products(group, got, back, owner, inner_id, res, psf, obs, mask, rm, rt, pm, pt)
            if group:
                wait_sends(gathering)
            copies[group] = send_rows(net, group, back, rows)
        zc, ring, cores = {}, [], []

        def done(q):
            if iteration < ITERS - 1:
                zc[q] = send_block(net, est, gz, q)
                return
            held[q, net.own] = est[q]
            cores.append(net.copy(held.at[q, net.own], held.at[q, net.own], "c", 1))
            for k in FAR:
                ring.append((q, k, net.copy(held.at[q, net.own], held.at[q, net.own], "y", k)))

        scatter(net, copies, back, rows, cum, core_out, core_in, ring_out, ring_own, ring_in,
                zout, zown, zin, est, tabs, done)
        if iteration < ITERS - 1:
            ahead = [cp for q in range(2) for cp in zc[q].values()]
            wait_sends([cp for cp in net.open if not any(cp is other for other in ahead)])
            net.open = ahead
            net.used = first
    for q, k, cp in ring:
        cp.wait_recv()
        there = ((net.y - k + NRING) % NRING) * 2 + net.c
        cores.append(net.copy(held.at[q, there], held.at[q, there], "c", 1))
    for cp in cores:
        cp.wait_recv()
    for q in range(2):
        for h in range(2):
            out[:, h * HALF + q * CH:h * HALF + (q + 1) * CH] = held[q, :, h * CH:(h + 1) * CH]
    wait_sends(net.open)


def twice(*shape_dtype):
    return [pltpu.VMEM(*shape_dtype)] * 2


SCRATCH = (
    [pltpu.VMEM((8, B), I32), pltpu.VMEM((2, NRING, 8, B), I32), pltpu.VMEM((8, B), I32), pltpu.SMEM((8, B), I32)]
    + twice((16, B, B), F32) + twice((16, B, B), BF) + twice((16, B, B), BF)
    + [pltpu.VMEM((REQ, EXPO, B, B), BF), pltpu.VMEM((2, HALF, B), F32), pltpu.VMEM((2, 8, HALF, B), F32)]
    + [pltpu.SemaphoreType.DMA((8,)), pltpu.SemaphoreType.DMA((SEMS,)), pltpu.SemaphoreType.DMA((SEMS,))]
    + [pltpu.VMEM((2, NZ, HALF, B), BF)]
    + twice((64, CH, B), BF) + twice((64, CH, B), BF) + twice((NRING, 2, REQ, CH, B), BF)
    + twice((NRING, 2, GROUP, CH, B), BF) + twice((NRING, 2, GROUP, CH, B), BF)
    + [pltpu.VMEM((REQ, B, B), BF)]
    + twice((NRING, REQ, HALF, B), BF) + twice((2, 64, CH, B), F32)
    + twice((2, NRING, NZ, CH, B), BF) + twice((2, NRING, NZ, CH, B), BF)
    + twice((2, NRING, NZ, CH, B), BF) + twice((2, NZ, CH, B), F32) + twice((2, NRING, NZ, CH, B), BF)
    + [pltpu.VMEM((2, NZ, HALF, B), BF), pltpu.VMEM((2, NZ, HALF, B), F32), pltpu.VMEM((2, NZ, HALF, B), BF)]
)


def on_device(sky, observed, src_owner, src_local, res_ids, psf_ids, pixel_mask, resample, psf):
    vm = pl.BlockSpec(memory_space=pltpu.VMEM)
    sm = pl.BlockSpec(memory_space=pltpu.SMEM)
    hbm = pl.BlockSpec(memory_space=pl.ANY)
    return pl.pallas_call(
        kernel, name="landweber",
        out_shape=jax.ShapeDtypeStruct((8, B, B), F32),
        in_specs=[sm, sm, sm, sm, vm, hbm, hbm, hbm, hbm], out_specs=vm,
        scratch_shapes=SCRATCH,
        compiler_params=pltpu.CompilerParams(
            collective_id=0, has_side_effects=True, vmem_limit_bytes=60 * 2**20),
    )(src_owner, src_local, jnp.swapaxes(res_ids, 1, 2)[0], jnp.swapaxes(psf_ids, 1, 2)[0], pixel_mask[0],
      sky, observed[0], resample, psf)


def solution(mesh):
    in_specs = (
        P("sky", None, None),
        P("exp", "sky", None, None, None),
        P("exp", "sky"),
        P("exp", "sky"),
        P("exp", "sky", None),
        P("exp", "sky", None),
        P("exp", "sky", None, None, None),
        P(),
        P(),
    )
    return jax.shard_map(
        on_device, mesh=mesh, in_specs=in_specs, out_specs=P("sky", None, None), check_vma=False
    )
```

```python
import jax
import jax.numpy as jnp
from jax import lax
from jax.experimental import pallas as pl
from jax.experimental.pallas import tpu as pltpu
from jax.sharding import PartitionSpec as P

MESH = pl.DeviceIdType.MESH
BF = jnp.bfloat16
F32 = jnp.float32
I32 = jnp.int32
ITERS = 2
NZ, NRING = 8, 4
B = 128
HALF = 64
NQ = 4
CH = HALF // NQ
REQ = 16
GROUP = 8
EXPO = 4
STEP = 1.0 / 128.0
ORDER = (0, 1, 3, 2)
POS = {0: 0, 1: 1, 3: 2, 2: 3}
FAR = (1, 3, 2)
NEAR = (1, 3, 2)
ZFAR = (4, 3, 5, 2, 6, 1, 7)
ZNEAR = (1, 7, 2, 6, 3, 5, 4)
HALVES = (("x", "y", 0), ("y", "x", HALF))
SEMS = 128


def at(z, x, y, c):
    return (z * NRING + x, y * 2 + c)


class Channel:
    def __init__(self, net, whole):
        self.net, self.whole, self.i = net, whole, net.used
        net.used += 1
        net.open.append(self)

    def _copy(self, src, dst, peer):
        return pltpu.make_async_remote_copy(
            src_ref=src, dst_ref=dst, send_sem=self.net.send.at[self.i], recv_sem=self.net.recv.at[self.i],
            device_id=peer, device_id_type=MESH)

    def copy(self, src, dst, axis, k):
        self._copy(src, dst, self.net.peers[axis, k]).start()

    def wait_recv(self):
        self._copy(self.whole, self.whole, self.net.peers["c", 1]).wait_recv()

    def wait_send(self):
        self._copy(self.whole, self.whole, self.net.peers["c", 1]).wait_send()


class Net:
    def __init__(self, send, recv):
        self.send, self.recv, self.used, self.open = send, recv, 0, []
        s, e = lax.axis_index("sky"), lax.axis_index("exp")
        self.z, self.x, self.y, self.c = z, x, y, c = s // NRING, s % NRING, e // 2, e % 2
        self.own = e
        self.peers = {("c", 1): at(z, x, y, 1 - c)}
        for k in FAR:
            self.peers["x", k] = at(z, (x + k) % NRING, y, c)
            self.peers["y", k] = at(z, x, (y + k) % NRING, c)
        for k in ZFAR:
            self.peers["z", k] = at((z + k) % NZ, x, y, c)

    def on(self, axis):
        return self.x if axis == "x" else self.y

    def barrier(self):
        bar = pltpu.get_barrier_semaphore()
        for peer in self.peers.values():
            pl.semaphore_signal(bar, inc=1, device_id=peer, device_id_type=MESH)
        pl.semaphore_wait(bar, len(self.peers))


def wait_sends(channels):
    for channel in channels:
        channel.wait_send()


def tables(net, seen, tab):
    lane = lax.broadcasted_iota(I32, (B, B), 1)
    sub = lax.broadcasted_iota(I32, (B, B), 0)
    for h in range(2):
        ids = sum(seen[h, k, POS[k]:POS[k] + 1, :] for k in range(NRING))
        zz, xx, yy, cc = ids // 32, (ids // 8) % 4, (ids // 2) % 4, ids % 2
        ring = xx if h == 0 else yy
        index = cc * 32 + ring * NZ + zz
        mine = (yy == net.y) if h == 0 else (xx == net.x)
        real = lane[0:1] < NRING * REQ
        key = jnp.broadcast_to(jnp.where(jnp.logical_and(mine, real), index, -1), (B, B))
        other = key.T
        earlier = jnp.logical_and(jnp.logical_and(key == other, key >= 0), sub < lane)
        tab[2 * h:2 * h + 1, :] = jnp.max(jnp.where(earlier, sub, -1), axis=0, keepdims=True)
        tab[2 * h + 1:2 * h + 2, :] = jnp.max(jnp.where(other == lane, sub, -1), axis=0, keepdims=True)
        tab[4 + h:5 + h, :] = index
    tab[6:8, :] = jnp.zeros((2, B), I32)


def id_tile(ids):
    lane = lax.broadcasted_iota(I32, (8, B), 1)
    sub = lax.broadcasted_iota(I32, (8, B), 0)
    tile = jnp.zeros((8, B), I32)
    for r, block in enumerate(ids):
        spot = (r // GROUP) * NRING * GROUP + sub * GROUP + r % GROUP
        tile = jnp.where(jnp.logical_and(lane == spot, sub < NRING), block, tile)
    return tile


def place(group, k, r):
    return group * NRING * GROUP + POS[k] * GROUP + r


def send_block(net, est, gz, q):
    gz[q, net.z] = est[q].astype(BF)
    channel = Channel(net, gz.at[q, pl.ds(0, NZ - 1)])
    for k in ZFAR:
        channel.copy(gz.at[q, net.z], gz.at[q, net.z], "z", k)
    return channel


def gather(net, zc, gz, full, slots, got, tabs):
    mid, cores, last = {}, {}, {}
    for q in range(NQ):
        zc[q].wait_recv()
        for h in range(2):
            mid[q, h] = Channel(net, full[h][q].at[pl.ds(0, 3 * NZ)])
        for k in FAR:
            for h, (dense, _, _) in enumerate(HALVES):
                here = pl.ds(net.c * 32 + net.on(dense) * NZ, NZ)
                mid[q, h].copy(gz.at[q, :, pl.ds(h * CH, CH)], full[h][q].at[here], dense, k)
        for h, (dense, _, _) in enumerate(HALVES):
            here = pl.ds(net.c * 32 + net.on(dense) * NZ, NZ)
            full[h][q][here] = gz[q, :, h * CH:(h + 1) * CH]

    def slot(group, chunks, send):
        for k in FAR + (0,):
            back_k = (NRING - k) % NRING

            def fill(r, carry):
                for h, (_, sparse, _) in enumerate(HALVES):
                    block = jnp.clip(tabs[4 + h, place(group, back_k, r)], 0, 63)
                    for q in chunks:
                        if k == 0:
                            got[h][group][net.on(sparse), q, r] = full[h][q][block]
                        else:
                            slots[h][k, q, group * GROUP + r] = full[h][q][block]
                return carry

            lax.fori_loop(0, GROUP, fill, 0, unroll=GROUP)
            if k:
                part, qs = pl.ds(group * GROUP, GROUP), pl.ds(chunks[0], len(chunks))
                for h, (_, sparse, _) in enumerate(HALVES):
                    send[h].copy(slots[h].at[k, qs, part], got[h][group].at[net.on(sparse), qs], sparse, k)

    for q in range(NQ):
        for h in range(2):
            mid[q, h].wait_recv()
            mine = pl.ds(net.c * 32, 32)
            cores[q, h] = Channel(net, full[h][q].at[pl.ds(0, 32)])
            cores[q, h].copy(full[h][q].at[mine], full[h][q].at[mine], "c", 1)
        if q == 0:
            last[0] = [Channel(net, got[h][0].at[pl.ds(0, 3)]) for h in range(2)]
        for h in range(2):
            cores[q, h].wait_recv()
        slot(0, (q,), last[0])
    last[1] = [Channel(net, got[h][1].at[pl.ds(0, 3)]) for h in range(2)]
    slot(1, tuple(range(NQ)), last[1])
    return last


def products(group, got, back, owner, inner_id, res, psf, obs, mask, rm, rt, pm, pt):
    def row(i):
        r = group * GROUP + i
        ysrc, xsrc = (inner_id[0, r] // 2) % NRING, owner[0, r] % NRING
        model = jnp.concatenate(
            [got[0][group][ysrc, q, i] for q in range(NQ)] + [got[1][group][xsrc, q, i] for q in range(NQ)], axis=0)
        r_ids = [res[x, r] for x in range(EXPO)]
        p_ids = [psf[x, r] for x in range(EXPO)]
        rows = jnp.concatenate([rm[i] for i in r_ids], axis=0)
        inner = jnp.dot(rows, model, preferred_element_type=F32).astype(BF)
        spread, cols = [], []
        for x in range(EXPO):
            predicted = jnp.dot(inner[x * B:(x + 1) * B], pt[p_ids[x]], preferred_element_type=F32)
            good = mask[r, x].astype(F32)
            resid = (predicted - obs[r, x].astype(F32)) * good[1:2]
            spread.append(jnp.dot(resid.astype(BF), pm[p_ids[x]], preferred_element_type=F32).astype(BF))
            cols.append(rt[r_ids[x]] * good[0:1].astype(BF))
        back[r] = jnp.dot(jnp.concatenate(cols, axis=1), jnp.concatenate(spread, axis=0),
                          preferred_element_type=F32).astype(BF)

    def two(i, carry):
        for j in range(4):
            row(4 * i + j)
        return carry

    lax.fori_loop(0, GROUP // 4, two, 0)


def send_rows(net, group, back, rows):
    part, copies = pl.ds(group * GROUP, GROUP), {}
    for q in range(NQ) if group else range(1):
        size, skip = (CH, q * CH) if group else (HALF, 0)
        for h in range(2):
            copies[q, h] = Channel(net, rows[h].at[pl.ds(0, 3), part, pl.ds(skip, size)])
        for k in FAR:
            for h, (_, sparse, lo) in enumerate(HALVES):
                copies[q, h].copy(back.at[part, pl.ds(lo + skip, size)],
                                  rows[h].at[k, part, pl.ds(skip, size)], sparse, k)
    return copies


def scatter(net, copies, back, rows, cum, core_out, core_in, ring_out, ring_own, ring_in,
            zout, zown, zin, est, tabs, done):
    def accumulate(group, chunks):
        for k in ORDER:
            if k == ORDER[1]:
                for q in chunks if group else range(1):
                    for h in range(2):
                        copies[group][q, h].wait_recv()

            def add(i, carry):
                p, r = place(group, k, i), group * GROUP + i
                for h, (_, _, lo) in enumerate(HALVES):
                    prev = tabs[2 * h, p]
                    for q in chunks:
                        if k == 0:
                            term = back[r, lo + q * CH:lo + (q + 1) * CH]
                        else:
                            term = rows[h][k, r, q * CH:(q + 1) * CH]
                        before = cum[h][q, jnp.clip(prev, 0, 63)]
                        cum[h][q, p] = term.astype(F32) + jnp.where(prev >= 0, before, 0.0)
                return carry

            lax.fori_loop(0, GROUP, add, 0, unroll=GROUP)

    def total(h, q, key):
        final = tabs[2 * h + 1, key]
        return jnp.where(final >= 0, cum[h][q, jnp.clip(final, 0, 63)], 0.0)

    cores, mids = {}, {}

    def to_core(q):
        for k in FAR + (0,):

            def pick(z, carry):
                for h, (dense, _, _) in enumerate(HALVES):
                    there = (net.on(dense) + k) % NRING
                    core_out[h][q, k, z] = total(h, q, (1 - net.c) * 32 + there * NZ + z).astype(BF)
                return carry

            lax.fori_loop(0, NZ, pick, 0, unroll=NZ)
        for h in range(2):
            cores[q, h] = Channel(net, core_in[h].at[q])
            cores[q, h].copy(core_out[h].at[q], core_in[h].at[q], "c", 1)

    def to_ring(q):
        for h in range(2):
            cores[q, h].wait_recv()
            mids[q, h] = Channel(net, ring_in[h].at[q, pl.ds(0, 3)])
        for k in FAR + (0,):

            def join(z, carry):
                for h, (dense, _, _) in enumerate(HALVES):
                    there = (net.on(dense) + k) % NRING
                    both = total(h, q, net.c * 32 + there * NZ + z) + core_in[h][q, k, z].astype(F32)
                    if k:
                        ring_out[h][q, k, z] = both.astype(BF)
                    else:
                        ring_own[h][q, z] = both
                return carry

            lax.fori_loop(0, NZ, join, 0, unroll=NZ)
            if k:
                for h, (dense, _, _) in enumerate(HALVES):
                    mids[q, h].copy(ring_out[h].at[q, k], ring_in[h].at[q, k], dense, k)

    accumulate(0, tuple(range(NQ)))
    for q in range(NQ):
        accumulate(1, (q,))
        to_core(q)
        if q:
            to_ring(q - 1)
    to_ring(NQ - 1)
    zc = {}
    for q in range(NQ):
        for h in range(2):
            mids[q, h].wait_recv()

        def ring(z, carry):
            for h in range(2):
                both = ring_own[h][q, z]
                for k in NEAR:
                    both = both + ring_in[h][q, k, z].astype(F32)
                zout[q, z, h * CH:(h + 1) * CH] = both.astype(BF)
                zown[q, z, h * CH:(h + 1) * CH] = both
            return carry

        lax.fori_loop(0, NZ, ring, 0, unroll=NZ)
        zc[q] = Channel(net, zin.at[q, pl.ds(0, NZ - 1)])
        for k in ZFAR:
            zc[q].copy(zout.at[q, (net.z + k) % NZ], zin.at[q, k], "z", k)
    for q in range(NQ):
        grad = zown[q, net.z]
        zc[q].wait_recv()
        for k in ZNEAR:
            grad = grad + zin[q, k].astype(F32)
        est[q] = jnp.maximum(est[q] - STEP * grad, 0.0)
        done(q)


def kernel(owner, inner_id, res, psf, mask, sky, observed, resample, psf_mats, out,
           idtile, seen, tab, tabs, r32, p32, rm, rt, pm, pt, obs, est, held, local, send, recv,
           gz, *rest):
    full = (rest[:NQ], rest[NQ:2 * NQ])
    (slots_a, slots_b, got_a0, got_a1, got_b0, got_b1, back, rows_a, rows_b, cum_a, cum_b,
     co_a, co_b, ci_a, ci_b, ro_a, ro_b, rw_a, rw_b, ri_a, ri_b, zout, zown, zin) = rest[2 * NQ:]
    got = ((got_a0, got_a1), (got_b0, got_b1))
    slots, rows = (slots_a, slots_b), (rows_a, rows_b)
    cum, core_out, core_in = (cum_a, cum_b), (co_a, co_b), (ci_a, ci_b)
    ring_out, ring_own, ring_in = (ro_a, ro_b), (rw_a, rw_b), (ri_a, ri_b)
    net = Net(send, recv)

    def fetch(src, dst, i):
        cp = pltpu.make_async_copy(src, dst, local.at[i])
        cp.start()
        return cp

    starts = [fetch(sky.at[net.own, pl.ds(h * HALF + q * CH, CH)], est.at[q, pl.ds(h * CH, CH)], h * NQ + q)
              for q in range(NQ) for h in range(2)]
    mats = [fetch(resample, r32, 8), fetch(psf_mats, p32, 9)]
    blocks = fetch(observed, obs, 10)
    own_ids = [owner[0, r] * 8 + inner_id[0, r] for r in range(REQ)]
    idtile[...] = id_tile(own_ids)
    net.barrier()
    told = []
    for h, (_, sparse, _) in enumerate(HALVES):
        told.append(Channel(net, seen.at[h, pl.ds(0, 3)]))
        for k in NEAR:
            told[h].copy(idtile, seen.at[h, k], sparse, k)
        seen[h, 0] = idtile[...]
    for cp in starts:
        cp.wait()
    zc = {q: send_block(net, est, gz, q) for q in range(NQ)}
    for cp in told:
        cp.wait_recv()
    tables(net, seen, tab)
    to_scalar = fetch(tab, tabs, 11)
    for cp in mats:
        cp.wait()

    def cast(i, carry):
        rm[i] = r32[i].astype(BF)
        rt[i] = r32[i].T.astype(BF)
        pm[i] = p32[i].astype(BF)
        pt[i] = p32[i].T.astype(BF)
        return carry

    lax.fori_loop(0, 16, cast, 0, unroll=2)
    to_scalar.wait()
    first = net.used
    for iteration in range(ITERS):
        last = gather(net, zc, gz, full, slots, got, tabs)
        if iteration == 0:
            blocks.wait()
        gathering, net.open = net.open, []
        copies = {}
        for group in range(2):
            for cp in last[group]:
                cp.wait_recv()
            products(group, got, back, owner, inner_id, res, psf, obs, mask, rm, rt, pm, pt)
            if group:
                wait_sends(gathering)
            copies[group] = send_rows(net, group, back, rows)
        zc, ring, cores = {}, [], []

        def done(q):
            if iteration < ITERS - 1:
                zc[q] = send_block(net, est, gz, q)
                return
            held[q, net.own] = est[q]
            mine = held.at[q, net.own]
            cores.append(Channel(net, mine))
            cores[-1].copy(mine, mine, "c", 1)
            for k in FAR:
                ring.append((q, k, Channel(net, mine)))
                ring[-1][2].copy(mine, mine, "y", k)

        scatter(net, copies, back, rows, cum, core_out, core_in, ring_out, ring_own, ring_in,
                zout, zown, zin, est, tabs, done)
        if iteration < ITERS - 1:
            ahead = [zc[q] for q in range(NQ)]
            wait_sends([cp for cp in net.open if not any(cp is other for other in ahead)])
            net.open = ahead
            net.used = first
    for q, k, cp in ring:
        cp.wait_recv()
        there = held.at[q, ((net.y - k + NRING) % NRING) * 2 + net.c]
        cores.append(Channel(net, there))
        cores[-1].copy(there, there, "c", 1)
    for cp in cores:
        cp.wait_recv()
    for q in range(NQ):
        for h in range(2):
            out[:, h * HALF + q * CH:h * HALF + (q + 1) * CH] = held[q, :, h * CH:(h + 1) * CH]
    wait_sends(net.open)


def twice(*shape_dtype):
    return [pltpu.VMEM(*shape_dtype)] * 2


SCRATCH = (
    [pltpu.VMEM((8, B), I32), pltpu.VMEM((2, NRING, 8, B), I32), pltpu.VMEM((8, B), I32), pltpu.SMEM((8, B), I32)]
    + twice((16, B, B), F32) + twice((16, B, B), BF) + twice((16, B, B), BF)
    + [pltpu.VMEM((REQ, EXPO, B, B), BF), pltpu.VMEM((NQ, 2 * CH, B), F32), pltpu.VMEM((NQ, 8, 2 * CH, B), F32)]
    + [pltpu.SemaphoreType.DMA((12,)), pltpu.SemaphoreType.DMA((SEMS,)), pltpu.SemaphoreType.DMA((SEMS,))]
    + [pltpu.VMEM((NQ, NZ, 2 * CH, B), BF)]
    + [pltpu.VMEM((64, CH, B), BF)] * (2 * NQ) + twice((NRING, NQ, REQ, CH, B), BF)
    + twice((NRING, NQ, GROUP, CH, B), BF) + twice((NRING, NQ, GROUP, CH, B), BF)
    + [pltpu.VMEM((REQ, B, B), BF)]
    + twice((NRING, REQ, HALF, B), BF) + twice((NQ, 64, CH, B), F32)
    + twice((NQ, NRING, NZ, CH, B), BF) + twice((NQ, NRING, NZ, CH, B), BF)
    + twice((NQ, NRING, NZ, CH, B), BF) + twice((NQ, NZ, CH, B), F32) + twice((NQ, NRING, NZ, CH, B), BF)
    + [pltpu.VMEM((NQ, NZ, 2 * CH, B), BF), pltpu.VMEM((NQ, NZ, 2 * CH, B), F32), pltpu.VMEM((NQ, NZ, 2 * CH, B), BF)]
)


def on_device(sky, observed, src_owner, src_local, res_ids, psf_ids, pixel_mask, resample, psf):
    vm = pl.BlockSpec(memory_space=pltpu.VMEM)
    sm = pl.BlockSpec(memory_space=pltpu.SMEM)
    hbm = pl.BlockSpec(memory_space=pl.ANY)
    return pl.pallas_call(
        kernel, name="landweber",
        out_shape=jax.ShapeDtypeStruct((8, B, B), F32),
        in_specs=[sm, sm, sm, sm, vm, hbm, hbm, hbm, hbm], out_specs=vm,
        scratch_shapes=SCRATCH,
        compiler_params=pltpu.CompilerParams(
            collective_id=0, has_side_effects=True, vmem_limit_bytes=60 * 2**20),
    )(src_owner, src_local, jnp.swapaxes(res_ids, 1, 2)[0], jnp.swapaxes(psf_ids, 1, 2)[0], pixel_mask[0],
      sky, observed[0], resample, psf)


def solution(mesh):
    in_specs = (
        P("sky", None, None),
        P("exp", "sky", None, None, None),
        P("exp", "sky"),
        P("exp", "sky"),
        P("exp", "sky", None),
        P("exp", "sky", None),
        P("exp", "sky", None, None, None),
        P(),
        P(),
    )
    return jax.shard_map(
        on_device, mesh=mesh, in_specs=in_specs, out_specs=P("sky", None, None), check_vma=False
    )
```

```python
import jax
import jax.numpy as jnp
from jax import lax
from jax.experimental import pallas as pl
from jax.experimental.pallas import tpu as pltpu
from jax.sharding import PartitionSpec as P

MESH = pl.DeviceIdType.MESH
BF = jnp.bfloat16
F32 = jnp.float32
I32 = jnp.int32
ITERS = 2
NZ, NRING = 8, 4
B = 128
HALF = 64
NQ = 4
CH = HALF // NQ
REQ = 16
GROUP = 8
EXPO = 4
STEP = 1.0 / 128.0
ORDER = (0, 1, 3, 2)
POS = {0: 0, 1: 1, 3: 2, 2: 3}
FAR = (1, 3, 2)
NEAR = (1, 3, 2)
ZFAR = (4, 3, 5, 2, 6, 1, 7)
ZNEAR = (1, 7, 2, 6, 3, 5, 4)
HALVES = (("x", "y", 0), ("y", "x", HALF))
SEMS = 128


def at(z, x, y, c):
    return (z * NRING + x, y * 2 + c)


class Channel:
    def __init__(self, net, whole):
        self.net, self.whole, self.i = net, whole, net.used
        net.used += 1
        net.open.append(self)

    def _copy(self, src, dst, peer):
        return pltpu.make_async_remote_copy(
            src_ref=src, dst_ref=dst, send_sem=self.net.send.at[self.i], recv_sem=self.net.recv.at[self.i],
            device_id=peer, device_id_type=MESH)

    def copy(self, src, dst, axis, k):
        self._copy(src, dst, self.net.peers[axis, k]).start()

    def wait_recv(self):
        self._copy(self.whole, self.whole, self.net.peers["c", 1]).wait_recv()

    def wait_send(self):
        self._copy(self.whole, self.whole, self.net.peers["c", 1]).wait_send()


class Net:
    def __init__(self, send, recv):
        self.send, self.recv, self.used, self.open = send, recv, 0, []
        s, e = lax.axis_index("sky"), lax.axis_index("exp")
        self.z, self.x, self.y, self.c = z, x, y, c = s // NRING, s % NRING, e // 2, e % 2
        self.own = e
        self.peers = {("c", 1): at(z, x, y, 1 - c)}
        for k in FAR:
            self.peers["x", k] = at(z, (x + k) % NRING, y, c)
            self.peers["y", k] = at(z, x, (y + k) % NRING, c)
        for k in ZFAR:
            self.peers["z", k] = at((z + k) % NZ, x, y, c)

    def on(self, axis):
        return self.x if axis == "x" else self.y

    def barrier(self):
        bar = pltpu.get_barrier_semaphore()
        for peer in self.peers.values():
            pl.semaphore_signal(bar, inc=1, device_id=peer, device_id_type=MESH)
        pl.semaphore_wait(bar, len(self.peers))


def wait_sends(channels):
    for channel in channels:
        channel.wait_send()


def tables(net, seen, tab):
    lane = lax.broadcasted_iota(I32, (B, B), 1)
    sub = lax.broadcasted_iota(I32, (B, B), 0)
    for h in range(2):
        ids = sum(seen[h, k, POS[k]:POS[k] + 1, :] for k in range(NRING))
        zz, xx, yy, cc = ids // 32, (ids // 8) % 4, (ids // 2) % 4, ids % 2
        ring = xx if h == 0 else yy
        index = cc * 32 + ring * NZ + zz
        mine = (yy == net.y) if h == 0 else (xx == net.x)
        real = lane[0:1] < NRING * REQ
        key = jnp.broadcast_to(jnp.where(jnp.logical_and(mine, real), index, -1), (B, B))
        other = key.T
        earlier = jnp.logical_and(jnp.logical_and(key == other, key >= 0), sub < lane)
        tab[2 * h:2 * h + 1, :] = jnp.max(jnp.where(earlier, sub, -1), axis=0, keepdims=True)
        tab[2 * h + 1:2 * h + 2, :] = jnp.max(jnp.where(other == lane, sub, -1), axis=0, keepdims=True)
        tab[4 + h:5 + h, :] = index
    tab[6:8, :] = jnp.zeros((2, B), I32)


def id_tile(ids):
    lane = lax.broadcasted_iota(I32, (8, B), 1)
    sub = lax.broadcasted_iota(I32, (8, B), 0)
    tile = jnp.zeros((8, B), I32)
    for r, block in enumerate(ids):
        spot = (r // GROUP) * NRING * GROUP + sub * GROUP + r % GROUP
        tile = jnp.where(jnp.logical_and(lane == spot, sub < NRING), block, tile)
    return tile


def place(group, k, r):
    return group * NRING * GROUP + POS[k] * GROUP + r


def send_block(net, est, gz, q):
    gz[q, net.z] = est[q].astype(BF)
    channel = Channel(net, gz.at[q, pl.ds(0, NZ - 1)])
    for k in ZFAR:
        channel.copy(gz.at[q, net.z], gz.at[q, net.z], "z", k)
    return channel


def gather(net, zc, gz, full, slots, got, tabs):
    mid, cores, last = {}, {}, {}
    for q in range(NQ):
        zc[q].wait_recv()
        for h in range(2):
            mid[q, h] = Channel(net, full[h][q].at[pl.ds(0, 3 * NZ)])
        for k in FAR:
            for h, (dense, _, _) in enumerate(HALVES):
                here = pl.ds(net.c * 32 + net.on(dense) * NZ, NZ)
                mid[q, h].copy(gz.at[q, :, pl.ds(h * CH, CH)], full[h][q].at[here], dense, k)
        for h, (dense, _, _) in enumerate(HALVES):
            here = pl.ds(net.c * 32 + net.on(dense) * NZ, NZ)
            full[h][q][here] = gz[q, :, h * CH:(h + 1) * CH]

    def slot(group, chunks, send):
        for k in FAR + (0,):
            back_k = (NRING - k) % NRING

            def fill(r, carry):
                for h, (_, sparse, _) in enumerate(HALVES):
                    block = jnp.clip(tabs[4 + h, place(group, back_k, r)], 0, 63)
                    for q in chunks:
                        if k == 0:
                            got[h][group][net.on(sparse), q, r] = full[h][q][block]
                        else:
                            slots[h][k, q, group * GROUP + r] = full[h][q][block]
                return carry

            lax.fori_loop(0, GROUP, fill, 0, unroll=GROUP)
            if k:
                part, qs = pl.ds(group * GROUP, GROUP), pl.ds(chunks[0], len(chunks))
                for h, (_, sparse, _) in enumerate(HALVES):
                    send[h].copy(slots[h].at[k, qs, part], got[h][group].at[net.on(sparse), qs], sparse, k)

    for q in range(NQ):
        for h in range(2):
            mid[q, h].wait_recv()
            mine = pl.ds(net.c * 32, 32)
            cores[q, h] = Channel(net, full[h][q].at[pl.ds(0, 32)])
            cores[q, h].copy(full[h][q].at[mine], full[h][q].at[mine], "c", 1)
        if q == 0:
            last[0] = [Channel(net, got[h][0].at[pl.ds(0, 3)]) for h in range(2)]
        for h in range(2):
            cores[q, h].wait_recv()
        slot(0, (q,), last[0])
    last[1] = [Channel(net, got[h][1].at[pl.ds(0, 3)]) for h in range(2)]
    slot(1, tuple(range(NQ)), last[1])
    return last


def products(group, got, back, owner, inner_id, res, psf, obs, mask, rm, rt, pm, pt):
    def row(i):
        r = group * GROUP + i
        ysrc, xsrc = (inner_id[0, r] // 2) % NRING, owner[0, r] % NRING
        model = jnp.concatenate(
            [got[0][group][ysrc, q, i] for q in range(NQ)] + [got[1][group][xsrc, q, i] for q in range(NQ)], axis=0)
        r_ids = [res[x, r] for x in range(EXPO)]
        p_ids = [psf[x, r] for x in range(EXPO)]
        rows = jnp.concatenate([rm[i] for i in r_ids], axis=0)
        inner = jnp.dot(rows, model, preferred_element_type=F32).astype(BF)
        spread, cols = [], []
        for x in range(EXPO):
            predicted = jnp.dot(inner[x * B:(x + 1) * B], pt[p_ids[x]], preferred_element_type=F32)
            good = mask[r, x].astype(F32)
            resid = (predicted - obs[r, x].astype(F32)) * good[1:2]
            spread.append(jnp.dot(resid.astype(BF), pm[p_ids[x]], preferred_element_type=F32).astype(BF))
            cols.append(rt[r_ids[x]] * good[0:1].astype(BF))
        back[r] = jnp.dot(jnp.concatenate(cols, axis=1), jnp.concatenate(spread, axis=0),
                          preferred_element_type=F32).astype(BF)

    def two(i, carry):
        for j in range(GROUP):
            row(j)
        return carry

    lax.fori_loop(0, 1, two, 0)


def send_rows(net, group, back, rows):
    part, copies = pl.ds(group * GROUP, GROUP), {}
    for q in range(NQ) if group else range(1):
        size, skip = (CH, q * CH) if group else (HALF, 0)
        for h in range(2):
            copies[q, h] = Channel(net, rows[h].at[pl.ds(0, 3), part, pl.ds(skip, size)])
        for k in FAR:
            for h, (_, sparse, lo) in enumerate(HALVES):
                copies[q, h].copy(back.at[part, pl.ds(lo + skip, size)],
                                  rows[h].at[k, part, pl.ds(skip, size)], sparse, k)
    return copies


def scatter(net, copies, back, rows, cum, core_out, core_in, ring_out, ring_own, ring_in,
            zout, zown, zin, est, tabs, done):
    def accumulate(group, chunks):
        for k in ORDER:
            if k == ORDER[1]:
                for q in chunks if group else range(1):
                    for h in range(2):
                        copies[group][q, h].wait_recv()

            def add(i, carry):
                p, r = place(group, k, i), group * GROUP + i
                for h, (_, _, lo) in enumerate(HALVES):
                    prev = tabs[2 * h, p]
                    for q in chunks:
                        if k == 0:
                            term = back[r, lo + q * CH:lo + (q + 1) * CH]
                        else:
                            term = rows[h][k, r, q * CH:(q + 1) * CH]
                        before = cum[h][q, jnp.clip(prev, 0, 63)]
                        cum[h][q, p] = term.astype(F32) + jnp.where(prev >= 0, before, 0.0)
                return carry

            lax.fori_loop(0, GROUP, add, 0, unroll=GROUP)

    def total(h, q, key):
        final = tabs[2 * h + 1, key]
        return jnp.where(final >= 0, cum[h][q, jnp.clip(final, 0, 63)], 0.0)

    cores, mids = {}, {}

    def to_core(q):
        for k in FAR + (0,):

            def pick(z, carry):
                for h, (dense, _, _) in enumerate(HALVES):
                    there = (net.on(dense) + k) % NRING
                    core_out[h][q, k, z] = total(h, q, (1 - net.c) * 32 + there * NZ + z).astype(BF)
                return carry

            lax.fori_loop(0, NZ, pick, 0, unroll=NZ)
        for h in range(2):
            cores[q, h] = Channel(net, core_in[h].at[q])
            cores[q, h].copy(core_out[h].at[q], core_in[h].at[q], "c", 1)

    def to_ring(q):
        for h in range(2):
            cores[q, h].wait_recv()
            mids[q, h] = Channel(net, ring_in[h].at[q, pl.ds(0, 3)])
        for k in FAR + (0,):

            def join(z, carry):
                for h, (dense, _, _) in enumerate(HALVES):
                    there = (net.on(dense) + k) % NRING
                    both = total(h, q, net.c * 32 + there * NZ + z) + core_in[h][q, k, z].astype(F32)
                    if k:
                        ring_out[h][q, k, z] = both.astype(BF)
                    else:
                        ring_own[h][q, z] = both
                return carry

            lax.fori_loop(0, NZ, join, 0, unroll=NZ)
            if k:
                for h, (dense, _, _) in enumerate(HALVES):
                    mids[q, h].copy(ring_out[h].at[q, k], ring_in[h].at[q, k], dense, k)

    accumulate(0, tuple(range(NQ)))
    for q in range(NQ):
        accumulate(1, (q,))
        to_core(q)
        if q:
            to_ring(q - 1)
    to_ring(NQ - 1)
    zc = {}
    for q in range(NQ):
        for h in range(2):
            mids[q, h].wait_recv()

        def ring(z, carry):
            for h in range(2):
                both = ring_own[h][q, z]
                for k in NEAR:
                    both = both + ring_in[h][q, k, z].astype(F32)
                zout[q, z, h * CH:(h + 1) * CH] = both.astype(BF)
                zown[q, z, h * CH:(h + 1) * CH] = both
            return carry

        lax.fori_loop(0, NZ, ring, 0, unroll=NZ)
        zc[q] = Channel(net, zin.at[q, pl.ds(0, NZ - 1)])
        for k in ZFAR:
            zc[q].copy(zout.at[q, (net.z + k) % NZ], zin.at[q, k], "z", k)
    for q in range(NQ):
        grad = zown[q, net.z]
        zc[q].wait_recv()
        for k in ZNEAR:
            grad = grad + zin[q, k].astype(F32)
        est[q] = jnp.maximum(est[q] - STEP * grad, 0.0)
        done(q)


def kernel(owner, inner_id, res, psf, mask, sky, observed, resample, psf_mats, out,
           idtile, seen, tab, tabs, r32, p32, rm, rt, pm, pt, obs, est, held, local, send, recv,
           gz, *rest):
    full = (rest[:NQ], rest[NQ:2 * NQ])
    (slots_a, slots_b, got_a0, got_a1, got_b0, got_b1, back, rows_a, rows_b, cum_a, cum_b,
     co_a, co_b, ci_a, ci_b, ro_a, ro_b, rw_a, rw_b, ri_a, ri_b, zout, zown, zin) = rest[2 * NQ:]
    got = ((got_a0, got_a1), (got_b0, got_b1))
    slots, rows = (slots_a, slots_b), (rows_a, rows_b)
    cum, core_out, core_in = (cum_a, cum_b), (co_a, co_b), (ci_a, ci_b)
    ring_out, ring_own, ring_in = (ro_a, ro_b), (rw_a, rw_b), (ri_a, ri_b)
    net = Net(send, recv)

    def fetch(src, dst, i):
        cp = pltpu.make_async_copy(src, dst, local.at[i])
        cp.start()
        return cp

    starts = [fetch(sky.at[net.own, pl.ds(h * HALF + q * CH, CH)], est.at[q, pl.ds(h * CH, CH)], h * NQ + q)
              for q in range(NQ) for h in range(2)]
    mats = [fetch(resample, r32, 8), fetch(psf_mats, p32, 9)]
    blocks = fetch(observed, obs, 10)
    own_ids = [owner[0, r] * 8 + inner_id[0, r] for r in range(REQ)]
    idtile[...] = id_tile(own_ids)
    net.barrier()
    told = []
    for h, (_, sparse, _) in enumerate(HALVES):
        told.append(Channel(net, seen.at[h, pl.ds(0, 3)]))
        for k in NEAR:
            told[h].copy(idtile, seen.at[h, k], sparse, k)
        seen[h, 0] = idtile[...]
    for cp in starts:
        cp.wait()
    zc = {q: send_block(net, est, gz, q) for q in range(NQ)}
    for cp in told:
        cp.wait_recv()
    tables(net, seen, tab)
    to_scalar = fetch(tab, tabs, 11)
    for cp in mats:
        cp.wait()

    def cast(i, carry):
        rm[i] = r32[i].astype(BF)
        rt[i] = r32[i].T.astype(BF)
        pm[i] = p32[i].astype(BF)
        pt[i] = p32[i].T.astype(BF)
        return carry

    lax.fori_loop(0, 16, cast, 0, unroll=2)
    to_scalar.wait()
    first = net.used
    for iteration in range(ITERS):
        last = gather(net, zc, gz, full, slots, got, tabs)
        if iteration == 0:
            blocks.wait()
        gathering, net.open = net.open, []
        copies = {}
        for group in range(2):
            for cp in last[group]:
                cp.wait_recv()
            products(group, got, back, owner, inner_id, res, psf, obs, mask, rm, rt, pm, pt)
            if group:
                wait_sends(gathering)
            copies[group] = send_rows(net, group, back, rows)
        zc, ring, cores = {}, [], []

        def done(q):
            if iteration < ITERS - 1:
                zc[q] = send_block(net, est, gz, q)
                return
            held[q, net.own] = est[q]
            mine = held.at[q, net.own]
            cores.append(Channel(net, mine))
            cores[-1].copy(mine, mine, "c", 1)
            for k in FAR:
                ring.append((q, k, Channel(net, mine)))
                ring[-1][2].copy(mine, mine, "y", k)

        scatter(net, copies, back, rows, cum, core_out, core_in, ring_out, ring_own, ring_in,
                zout, zown, zin, est, tabs, done)
        if iteration < ITERS - 1:
            ahead = [zc[q] for q in range(NQ)]
            wait_sends([cp for cp in net.open if not any(cp is other for other in ahead)])
            net.open = ahead
            net.used = first
    for q, k, cp in ring:
        cp.wait_recv()
        there = held.at[q, ((net.y - k + NRING) % NRING) * 2 + net.c]
        cores.append(Channel(net, there))
        cores[-1].copy(there, there, "c", 1)
    for cp in cores:
        cp.wait_recv()
    for q in range(NQ):
        for h in range(2):
            out[:, h * HALF + q * CH:h * HALF + (q + 1) * CH] = held[q, :, h * CH:(h + 1) * CH]
    wait_sends(net.open)


def twice(*shape_dtype):
    return [pltpu.VMEM(*shape_dtype)] * 2


SCRATCH = (
    [pltpu.VMEM((8, B), I32), pltpu.VMEM((2, NRING, 8, B), I32), pltpu.VMEM((8, B), I32), pltpu.SMEM((8, B), I32)]
    + twice((16, B, B), F32) + twice((16, B, B), BF) + twice((16, B, B), BF)
    + [pltpu.VMEM((REQ, EXPO, B, B), BF), pltpu.VMEM((NQ, 2 * CH, B), F32), pltpu.VMEM((NQ, 8, 2 * CH, B), F32)]
    + [pltpu.SemaphoreType.DMA((12,)), pltpu.SemaphoreType.DMA((SEMS,)), pltpu.SemaphoreType.DMA((SEMS,))]
    + [pltpu.VMEM((NQ, NZ, 2 * CH, B), BF)]
    + [pltpu.VMEM((64, CH, B), BF)] * (2 * NQ) + twice((NRING, NQ, REQ, CH, B), BF)
    + twice((NRING, NQ, GROUP, CH, B), BF) + twice((NRING, NQ, GROUP, CH, B), BF)
    + [pltpu.VMEM((REQ, B, B), BF)]
    + twice((NRING, REQ, HALF, B), BF) + twice((NQ, 64, CH, B), F32)
    + twice((NQ, NRING, NZ, CH, B), BF) + twice((NQ, NRING, NZ, CH, B), BF)
    + twice((NQ, NRING, NZ, CH, B), BF) + twice((NQ, NZ, CH, B), F32) + twice((NQ, NRING, NZ, CH, B), BF)
    + [pltpu.VMEM((NQ, NZ, 2 * CH, B), BF), pltpu.VMEM((NQ, NZ, 2 * CH, B), F32), pltpu.VMEM((NQ, NZ, 2 * CH, B), BF)]
)


def on_device(sky, observed, src_owner, src_local, res_ids, psf_ids, pixel_mask, resample, psf):
    vm = pl.BlockSpec(memory_space=pltpu.VMEM)
    sm = pl.BlockSpec(memory_space=pltpu.SMEM)
    hbm = pl.BlockSpec(memory_space=pl.ANY)
    return pl.pallas_call(
        kernel, name="landweber",
        out_shape=jax.ShapeDtypeStruct((8, B, B), F32),
        in_specs=[sm, sm, sm, sm, vm, hbm, hbm, hbm, hbm], out_specs=vm,
        scratch_shapes=SCRATCH,
        compiler_params=pltpu.CompilerParams(
            collective_id=0, has_side_effects=True, vmem_limit_bytes=60 * 2**20),
    )(src_owner, src_local, jnp.swapaxes(res_ids, 1, 2)[0], jnp.swapaxes(psf_ids, 1, 2)[0], pixel_mask[0],
      sky, observed[0], resample, psf)


def solution(mesh):
    in_specs = (
        P("sky", None, None),
        P("exp", "sky", None, None, None),
        P("exp", "sky"),
        P("exp", "sky"),
        P("exp", "sky", None),
        P("exp", "sky", None),
        P("exp", "sky", None, None, None),
        P(),
        P(),
    )
    return jax.shard_map(
        on_device, mesh=mesh, in_specs=in_specs, out_specs=P("sky", None, None), check_vma=False
    )
```
